128 devices in a mesh: section: 2 (over z_lo), fsdp: 16 (over z_hi, y, core), rep: 4 (over x).
Axes of the slice: x: 4, y: 4, z: 4 (z_hi: 2, z_lo: 2; z = z_hi * 2 + z_lo), core: 2. Of those that a mesh axis runs over, the one named last changes fastest.
Arguments:
- layer_input: bfloat16 [2, 4, 1024, 1024], P(None, 'rep', 'fsdp'), may hold values from -6 to 6
- cotangent: bfloat16 [2, 4, 1024, 1024], P(None, 'rep', 'fsdp'), may hold values from -6 to 6
- seq_lengths: int32 [2, 4, 4], P(None, 'rep'), may hold values from 0 to 1024, as said below
- norm_gains: bfloat16 [2, 2, 1024], P('section', None, 'fsdp'), may hold values from 0.099609375 to 1.8984375
- w_mix: bfloat16 [2, 1024, 4096], P('section', 'fsdp'), may hold values from -0.1875 to 0.1875
- w_step: bfloat16 [2, 1024, 24], P('section', 'fsdp'), may hold values from -0.1875 to 0.1875
- conv_kernel: bfloat16 [2, 4, 1792], P('section', None, 'fsdp'), may hold values from -3 to 3
- conv_bias: bfloat16 [2, 1792], P('section', 'fsdp'), may hold values from -3 to 3
- head_params: float32 [2, 3, 24], P('section'), may hold values from -13 to 1.5, as said below
- w_out: bfloat16 [2, 2048, 1024], P('section', 'fsdp'), may hold values from -0.25 to 0.25
- w_gate_up: bfloat16 [2, 1024, 4096], P('section', 'fsdp'), may hold values from -0.1875 to 0.1875
- w_down: bfloat16 [2, 2048, 1024], P('section', 'fsdp'), may hold values from -0.125 to 0.125
Outputs:
- activations: bfloat16 [2, 2, 4, 1024, 1024], P('section', None, 'rep', 'fsdp')
- input_grad: float32 [2, 2, 4, 1024, 1024], P('section', None, 'rep', 'fsdp')
- grad_norm_gains: float32 [2, 2, 1024], P('section', None, 'fsdp')
- grad_w_mix: float32 [2, 1024, 4096], P('section', 'fsdp')
- grad_w_step: float32 [2, 1024, 24], P('section', 'fsdp')
- grad_conv_kernel: float32 [2, 4, 1792], P('section', None, 'fsdp')
- grad_conv_bias: float32 [2, 1792], P('section', 'fsdp')
- grad_head_params: float32 [2, 3, 24], P('section')
- grad_w_out: float32 [2, 2048, 1024], P('section', 'fsdp')
- grad_w_gate_up: float32 [2, 1024, 4096], P('section', 'fsdp')
- grad_w_down: float32 [2, 2048, 1024], P('section', 'fsdp')
The draws below stay inside these ranges and needn't reach their ends.
Inputs may be any that keep to these rules, and one draw needn't show every extreme that they name: `seq_lengths`: in each pack the sequences, each padded up to whole blocks of 64 tokens, take at most 1024 tokens together, and at least one slot is used; in each group one micro-batch holds a single sequence of 1024 tokens. `head_params`: row 2 (skip gains) lies in 0.5 to 1.5, row 1 (log rates) in -0.5 to 0.5.
All inputs are finite; a program needn't handle non-finite values.
Results may differ from the reference program's by a relative error of at most 0.025.
Values may be sent and summed in bfloat16 or wider, within the bound.
No kernel may reach another device: no remote copies, remote signals or barrier semaphores. Data moves between devices by JAX's collectives and lax.ppermute only.
A program may use at most 256 MiB of HBM per device.

```python
import math
import jax
import jax.numpy as jnp
from jax import lax

D = 1024
QUERY_HEADS = 8
KEY_VALUE_HEADS = 2
HEAD_SIZE = 64
MIXER_HEADS = 24
MIXER_HEAD_SIZE = 64
STATE_SIZE = 128
KC = 4
FF = 2048
MICRO = 2
SLOTS = 4
BLK = 64
PACK = 1024
GROUPS = 4
SPACE_CHANNELS = 1536
XBC = 1792
MIXW = 4096
OUTW = 2048
N_SECTION = 2
N_FSDP = 16


def draw_seq_lengths(key, part):
    key = jax.random.fold_in(key, 7)
    keys_list = jax.random.split(key, 4)
    share_blocks = N_FSDP // SLOTS
    blocks_used = jax.random.randint(keys_list[0], (MICRO, GROUPS, SLOTS), 0, share_blocks + 1)
    leading = jax.random.randint(keys_list[1], (MICRO, GROUPS, 1), 1, share_blocks + 1)
    blocks_used = jnp.concatenate([leading, blocks_used[:, :, 1:]], axis=2)
    tail_rows = jax.random.randint(keys_list[2], (MICRO, GROUPS, SLOTS), 1, BLK + 1)
    ragged = jnp.where(blocks_used > 0, (blocks_used - 1) * BLK + tail_rows, 0)
    full_micro = jax.random.randint(keys_list[3], (1, GROUPS, 1), 0, MICRO)
    micro_order = jnp.arange(MICRO, dtype=jnp.int32)[:, None, None]
    slot_order = jnp.arange(SLOTS, dtype=jnp.int32)[None, None, :]
    full_row = jnp.where(slot_order == 0, PACK, 0)
    return jnp.where(micro_order == full_micro, full_row, ragged).astype(jnp.int32)


def draw_head_params(key, part):
    key = jax.random.fold_in(key, 11)
    keys_list = jax.random.split(key, 3)
    slow_rate = 0.5 / PACK
    fast_rate = 1.0 / 30.0
    log_rates = jax.random.uniform(keys_list[0], (N_SECTION, MIXER_HEADS), jnp.float32, math.log(slow_rate), math.log(fast_rate))
    decay_logs = jax.random.uniform(keys_list[1], (N_SECTION, MIXER_HEADS), jnp.float32, -0.5, 0.5)
    skip_gains = jax.random.uniform(keys_list[2], (N_SECTION, MIXER_HEADS), jnp.float32, 0.5, 1.5)
    return jnp.stack([log_rates - decay_logs, decay_logs, skip_gains], axis=1).astype(jnp.float32)


def levels(own_key, extent, shards, least, largest):
    factor_of = 1.0
    for axis_at, parts in shards:
        steps = jax.random.uniform(jax.random.fold_in(jax.random.fold_in(own_key, 6), axis_at), (parts,), jnp.float32, least / len(shards), largest / len(shards))
        factor_of = factor_of * jnp.repeat(jnp.exp(steps), extent[axis_at] // parts).reshape((-1,) + (1,) * (len(extent) - 1 - axis_at))
    return factor_of


def bell_draw(rng, shape, deviation, most, shards=(), kind=jnp.bfloat16):
    values = jax.random.normal(rng, shape, jnp.float32) * deviation
    if len(shards) > 0:
        values = levels(rng, shape, shards, -0.22, 0.18) * values
    return jnp.clip(values, min=-most, max=most).astype(kind)


def setup_inputs(seed: int = 0) -> dict:
    keys = jax.random.split(jax.random.key(seed), 13)
    return {
        "layer_input": bell_draw(keys[0], (MICRO, GROUPS, PACK, D), 1.0, 6.0, ((1, 4), (2, 16))),
        "cotangent": bell_draw(keys[1], (MICRO, GROUPS, PACK, D), 1.0, 6.0, ((1, 4), (2, 16))),
        "seq_lengths": draw_seq_lengths(jax.random.fold_in(keys[12], 71), 0),
        "norm_gains": jnp.clip(1.0 + 0.18 * jax.random.normal(keys[3], (N_SECTION, 2, D), jnp.float32), 0.099609375, 1.8984375).astype(jnp.bfloat16),
        "w_mix": bell_draw(keys[4], (N_SECTION, D, MIXW), D ** -0.5, 0.1875, ((0, 2), (1, 16))),
        "w_step": bell_draw(keys[5], (N_SECTION, D, MIXER_HEADS), D ** -0.5, 0.1875, ((0, 2), (1, 16))),
        "conv_kernel": bell_draw(keys[6], (N_SECTION, KC, XBC), KC ** -0.5, 3.0, ((0, 2), (2, 16))),
        "conv_bias": bell_draw(keys[7], (N_SECTION, XBC), 0.5, 3.0, ((0, 2), (1, 16))),
        "head_params": draw_head_params(jax.random.fold_in(keys[12], 71), 0),
        "w_out": bell_draw(keys[9], (N_SECTION, OUTW, D), (OUTW // 4) ** -0.5, 0.25, ((0, 2), (1, 16))),
        "w_gate_up": bell_draw(keys[10], (N_SECTION, D, 2 * FF), D ** -0.5, 0.1875, ((0, 2), (1, 16))),
        "w_down": bell_draw(keys[11], (N_SECTION, FF, D), FF ** -0.5, 0.125, ((0, 2), (1, 16))),
    }


rope_base = 100000000000.0
norm_epsilon = 1e-05
masked_score = -1e+30

@jax.custom_vjp
def lower_precision(v):
    return lax.optimization_barrier(v.astype(jnp.bfloat16)).astype(jnp.float32)

@jax.custom_vjp
def low_back(v):
    return v

def low_keep(v):
    return (lower_precision(v), None)

def low_pass(kept, grad):
    return (grad,)

def back_keep(v):
    return (v, None)

def back_low(kept, grad):
    return (lower_precision(grad),)
lower_precision.defvjp(low_keep, low_pass)
low_back.defvjp(back_keep, back_low)

def matmul(left, right):
    return jnp.dot(left, right, precision=lax.Precision.HIGHEST, preferred_element_type=jnp.float32)

def norm_rows(value_rows, gain):
    return value_rows * lax.rsqrt(lax.optimization_barrier(jnp.mean(value_rows * value_rows, axis=-1, keepdims=True)) + norm_epsilon) * gain

def rotary_angles(value_rows, token_positions):
    half_width = value_rows.shape[-1] // 2
    frequency = rope_base ** (-jnp.arange(half_width, dtype=jnp.float32) / half_width)
    angles = token_positions.astype(jnp.float32)[:, None] * frequency[None, :]
    cosine = jnp.cos(angles)[:, None, :]
    sine_part = jnp.sin(angles)[:, None, :]
    first_half = value_rows[..., :half_width]
    second_half = value_rows[..., half_width:]
    return jnp.concatenate([first_half * cosine - second_half * sine_part, second_half * cosine + first_half * sine_part], axis=-1)

def pack_layout(lengths_row, count_of_blocks, rows_per_block):
    used_blocks = ((lengths_row + rows_per_block - 1) // rows_per_block).astype(jnp.int32)
    first_block = (jnp.cumsum(used_blocks) - used_blocks).astype(jnp.int32)
    block_order = jnp.arange(count_of_blocks, dtype=jnp.int32)
    covers = ((block_order[:, None] >= first_block[None, :]) & (block_order[:, None] < (first_block + used_blocks)[None, :])).astype(jnp.int32)
    occupied = lax.optimization_barrier(jnp.sum(covers, axis=1)) > 0
    slot_order = jnp.arange(lengths_row.shape[0], dtype=jnp.int32)
    segment = jnp.where(occupied, lax.optimization_barrier(jnp.sum(covers * slot_order[None, :], axis=1)), -1).astype(jnp.int32)
    begins = lax.optimization_barrier(jnp.sum(covers * first_block[None, :], axis=1)).astype(jnp.int32)
    seq_length = lax.optimization_barrier(jnp.sum(covers * lengths_row[None, :], axis=1)).astype(jnp.int32)
    within = ((block_order - begins)[:, None] * rows_per_block + jnp.arange(rows_per_block, dtype=jnp.int32)[None, :]).astype(jnp.int32)
    is_valid = occupied[:, None] & (within < seq_length[:, None])
    carry_flag = occupied & (block_order > begins)
    return (segment, within, is_valid, carry_flag)

def allowed_mask(segment, is_valid, query_start, rows_of_queries):
    rows_per_block = is_valid.shape[1]
    token_segment = jnp.repeat(segment, rows_per_block)
    token_valid = is_valid.reshape(-1)
    key_order = jnp.arange(token_valid.shape[0], dtype=jnp.int32)
    query_order = query_start + jnp.arange(rows_of_queries, dtype=jnp.int32)
    query_segment = lax.dynamic_slice_in_dim(token_segment, query_start, rows_of_queries, 0)
    same_sequence = (query_segment[:, None] == token_segment[None, :]) & (key_order[None, :] <= query_order[:, None]) & token_valid[None, :]
    return same_sequence | (key_order[None, :] == query_order[:, None])

def conv_apply(extended, kernel, offset):
    out_rows = extended.shape[-2] - kernel.shape[0] + 1
    total_sum = offset
    for tap in range(kernel.shape[0]):
        total_sum = total_sum + kernel[tap] * extended[..., tap:tap + out_rows, :]
    return jax.nn.silu(total_sum)

def block_decay(step, decay_log):
    return jnp.cumsum(step * (-jnp.exp(decay_log))[None, :], axis=0)

def block_output(state_inputs, input_b, output_c, step, decay_log, skip_gain, incoming):
    cumul = block_decay(step, decay_log)
    count_of_rows = state_inputs.shape[0]
    causal = (jnp.arange(count_of_rows)[:, None] >= jnp.arange(count_of_rows)[None, :])[:, :, None]
    gaps = cumul[:, None, :] - cumul[None, :, :]
    decay = jnp.where(causal, jnp.exp(jnp.where(causal, gaps, 0.0)), 0.0)
    intersection = jnp.dot(output_c, input_b.T, precision=lax.Precision.HIGHEST)
    mixing = intersection[:, :, None] * decay * step[None, :, :]
    inner = jnp.einsum('tsh,shp->thp', mixing, state_inputs, precision=lax.Precision.HIGHEST)
    carried = jnp.einsum('tn,hpn->thp', output_c, incoming, precision=lax.Precision.HIGHEST) * jnp.exp(cumul)[:, :, None]
    return inner + carried + skip_gain[None, :, None] * state_inputs

def block_state(state_inputs, input_b, step, decay_log):
    cumul = block_decay(step, decay_log)
    tail = jnp.exp(cumul[-1][None, :] - cumul) * step
    local_state = jnp.einsum('sh,shp,sn->hpn', tail, state_inputs, input_b, precision=lax.Precision.HIGHEST)
    return (local_state, jnp.exp(cumul[-1]))

def chain_step(carried, block_items):
    local_state, decay_total, carry_flag = block_items
    arriving = carried * carry_flag
    return (decay_total[:, None, None] * arriving + local_state, arriving)

def pack_attention(query_vectors, key_rows, value_rows, allowed):
    count_of_tokens = query_vectors.shape[0]
    grouped_heads = query_vectors.reshape(count_of_tokens, KEY_VALUE_HEADS, QUERY_HEADS // KEY_VALUE_HEADS, HEAD_SIZE)
    raw_scores = low_back(jnp.einsum('qgrd,kgd->grqk', grouped_heads, key_rows, precision=lax.Precision.HIGHEST))
    scores = jnp.where(allowed[None, None], raw_scores * HEAD_SIZE ** (-0.5), masked_score)
    probs = lower_precision(jax.nn.softmax(scores, axis=-1))
    attended = jnp.einsum('grqk,kgd->qgrd', probs, value_rows, precision=lax.Precision.HIGHEST)
    return attended.reshape(count_of_tokens, QUERY_HEADS * HEAD_SIZE)

def mixer_layer(params, layer_in, segment, within, is_valid, carry_flag):
    gains, mix_weight, step_weight, conv_weight, conv_offset, heads, out_weight, gate_up_weight, down_weight = params
    count_of_tokens = layer_in.shape[0]
    count_of_blocks = segment.shape[0]
    rows_per_block = count_of_tokens // count_of_blocks
    token_positions = within.reshape(-1)
    normed = lower_precision(norm_rows(layer_in, gains[0]))
    mixed_rows = low_back(matmul(normed, mix_weight))
    step_raw = low_back(matmul(normed, step_weight))
    gate_z = mixed_rows[:, :SPACE_CHANNELS]
    conv_in = lower_precision(mixed_rows[:, SPACE_CHANNELS:SPACE_CHANNELS + XBC])
    attention_offset = SPACE_CHANNELS + XBC
    query_vectors = lower_precision(rotary_angles(mixed_rows[:, attention_offset:attention_offset + QUERY_HEADS * HEAD_SIZE].reshape(count_of_tokens, QUERY_HEADS, HEAD_SIZE), token_positions))
    key_rows = lower_precision(rotary_angles(mixed_rows[:, attention_offset + QUERY_HEADS * HEAD_SIZE:attention_offset + (QUERY_HEADS + KEY_VALUE_HEADS) * HEAD_SIZE].reshape(count_of_tokens, KEY_VALUE_HEADS, HEAD_SIZE), token_positions))
    value_rows = lower_precision(mixed_rows[:, attention_offset + (QUERY_HEADS + KEY_VALUE_HEADS) * HEAD_SIZE:].reshape(count_of_tokens, KEY_VALUE_HEADS, HEAD_SIZE))
    allowed = allowed_mask(segment, is_valid, 0, count_of_tokens)
    attended = jax.checkpoint(pack_attention)(query_vectors, key_rows, value_rows, allowed)
    blocked = conv_in.reshape(count_of_blocks, rows_per_block, XBC)
    edges = jnp.concatenate([jnp.zeros((1, KC - 1, XBC), jnp.float32), blocked[:-1, rows_per_block - KC + 1:]], axis=0)
    extended = jnp.concatenate([edges * carry_flag.astype(jnp.float32)[:, None, None], blocked], axis=1)
    activated_rows = conv_apply(extended, conv_weight, conv_offset)
    state_inputs = activated_rows[..., :SPACE_CHANNELS].reshape(count_of_blocks, rows_per_block, MIXER_HEADS, MIXER_HEAD_SIZE)
    input_b = activated_rows[..., SPACE_CHANNELS:SPACE_CHANNELS + STATE_SIZE]
    output_c = activated_rows[..., SPACE_CHANNELS + STATE_SIZE:]
    step = jax.nn.softplus(step_raw + heads[0]).reshape(count_of_blocks, rows_per_block, MIXER_HEADS)
    local_states, decay_totals = jax.vmap(block_state, in_axes=(0, 0, 0, None))(state_inputs, input_b, step, heads[1])
    initial_state = jnp.zeros((MIXER_HEADS, MIXER_HEAD_SIZE, STATE_SIZE), jnp.float32)
    _, incomings = lax.scan(chain_step, initial_state, (local_states, decay_totals, carry_flag.astype(jnp.float32)))
    ssm_out = jax.vmap(block_output, in_axes=(0, 0, 0, 0, None, None, 0))(state_inputs, input_b, output_c, step, heads[1], heads[2], incomings)
    gated = ssm_out.reshape(count_of_tokens, SPACE_CHANNELS) * jax.nn.silu(gate_z)
    joined = lower_precision(jnp.concatenate([low_back(attended), gated], axis=1))
    resid = layer_in + low_back(matmul(joined, out_weight))
    normed_two = lower_precision(norm_rows(resid, gains[1]))
    gate_up = low_back(matmul(normed_two, gate_up_weight))
    hidden = lower_precision(jax.nn.silu(gate_up[:, :FF]) * gate_up[:, FF:])
    ffn_out = low_back(matmul(hidden, down_weight))
    return is_valid.reshape(count_of_tokens, 1).astype(jnp.float32) * (resid + ffn_out)

def reference(layer_input, cotangent, seq_lengths, norm_gains, w_mix, w_step, conv_kernel, conv_bias, head_params, w_out, w_gate_up, w_down):
    weights = tuple((weight.astype(jnp.float32) for weight in (norm_gains, w_mix, w_step, conv_kernel, conv_bias, head_params, w_out, w_gate_up, w_down)))
    pack_total = MICRO * GROUPS
    base = layer_input.astype(jnp.float32).reshape(pack_total, PACK, D)
    layouts = jax.vmap(lambda lengths_row: pack_layout(lengths_row, N_FSDP, BLK))(seq_lengths.reshape(pack_total, SLOTS))

    def run_section(params, section_in):

        def one_pack(items):
            return mixer_layer(params, items[0], items[1], items[2], items[3], items[4])
        return lax.map(one_pack, (section_in, layouts[0], layouts[1], layouts[2], layouts[3]))

    def forward(weight_set, first_in, probes):
        outputs = []
        section_in = first_in
        for section_number in range(N_SECTION):
            params = tuple((weight[section_number] for weight in weight_set))
            if section_number > 0:
                section_in = low_back(outputs[-1]) + probes[section_number - 1]
            outputs.append(lower_precision(run_section(params, section_in)))
        return tuple(outputs)
    probes = jnp.zeros((N_SECTION - 1, pack_total, PACK, D), jnp.float32)
    section_outs, pullback = jax.vjp(forward, weights, base, probes)
    cotangents = tuple((jnp.zeros_like(item) for item in section_outs[:-1])) + (cotangent.astype(jnp.float32).reshape(pack_total, PACK, D),)
    weight_grads, base_grad, probe_grads = pullback(cotangents)
    activations = jnp.stack(section_outs).reshape(N_SECTION, MICRO, GROUPS, PACK, D).astype(jnp.bfloat16)
    input_grad = jnp.concatenate([base_grad[None], probe_grads], axis=0).reshape(N_SECTION, MICRO, GROUPS, PACK, D)
    return (activations, input_grad, weight_grads[0], weight_grads[1], weight_grads[2], weight_grads[3], weight_grads[4], weight_grads[5], weight_grads[6], weight_grads[7], weight_grads[8])
```

```python
import jax
import jax.numpy as jnp
import numpy as np
from jax import lax
from jax.experimental import pallas as pl
from jax.experimental.pallas import tpu as pltpu
from jax.sharding import Mesh
from jax.sharding import PartitionSpec as P

QUERY_HEADS = 8
KEY_VALUE_HEADS = 2
HEAD_SIZE = 64
MIXER_HEADS = 24
STATE_SIZE = 128
KC = 4
FF = 2048
SPACE_CHANNELS = 1536
XBC = 1792
BLOCK = 64

TEAM = 8
HALVES = 2
HEADS = MIXER_HEADS // TEAM
CH = SPACE_CHANNELS // TEAM
CONV = CH + 2 * STATE_SIZE
SEQ = 512
COLS = 896
STEP_AT = 2 * CH + 2 * STATE_SIZE + 3 * HEAD_SIZE
SMALL_AT = STEP_AT + HEADS
HID = FF // TEAM

rope_base = 100000000000.0
norm_epsilon = 1e-05
masked_score = -1e30
bf = jnp.bfloat16
f32 = jnp.float32


def mm(left, right):
    return jnp.dot(left, right, preferred_element_type=f32)


def mm_t(left, right):
    return lax.dot_general(left, right, (((1,), (1,)), ((), ())), preferred_element_type=f32)


def t_mm(left, right):
    return lax.dot_general(left, right, (((0,), (0,)), ((), ())), preferred_element_type=f32)


def after(x, *others):
    return lax.optimization_barrier((x, others))[0]


def shifted(x, axis, by, devices):
    return lax.ppermute(x, axis, [(i, (i + by) % devices) for i in range(devices)])


def swap(x, axis):
    return lax.ppermute(x, axis, [(0, 1), (1, 0)])


def gather_ring(x, axis):
    devices = 4
    parts = jnp.stack([x] + [shifted(x, axis, by, devices) for by in range(1, devices)])
    order = (lax.axis_index(axis) - jnp.arange(devices)) % devices
    return parts[order]


RING = ("section", "zhi")
FORWARD = [(0, 2), (2, 1), (1, 3), (3, 0)]
BACKWARD = [(b, a) for a, b in FORWARD]


def around(x):
    half = x.shape[0] // 2
    behind = lax.ppermute(x, RING, FORWARD)
    ahead = lax.ppermute(x, RING, BACKWARD)
    far = (
        lax.ppermute(behind[:half], RING, FORWARD),
        lax.ppermute(ahead[half:], RING, BACKWARD),
    )
    return x, jnp.concatenate(far), behind, ahead


def place_of_unit(unit):
    return (unit, 0) if unit < 8 else ((unit - 8) // 3, 1 + (unit - 8) % 3)


def unit_routes():
    edges = []
    for unit in range(32):
        team, slot = place_of_unit(unit)
        for half in range(2):
            edges.append((unit // 2, half * 8 + team, unit % 2, slot))
    routes = []
    left = list(edges)
    while left:
        taken = {}

        def place(source, seen):
            for e in left:
                if e[0] != source or e[1] in seen:
                    continue
                seen.add(e[1])
                if e[1] not in taken or place(taken[e[1]][0], seen):
                    taken[e[1]] = e
                    return True
            return False

        for source in range(16):
            place(source, set())
        chosen = sorted(taken.values())
        routes.append(chosen)
        for e in chosen:
            left.remove(e)
    return routes


ROUTES = unit_routes()
UNIT_AXES = ("zhi", "y", "core")


def device_table():
    table = np.zeros((16, 30), np.int32)
    for at in range(16):
        table[at, :3] = (at % 8) // 2, at % 2, at // 8
    for r, route in enumerate(ROUTES):
        for source, dest, unit, slot in route:
            table[source, 4 + r] = unit
            table[dest, 8 + r] = slot
    for at in range(16):
        half, member = at // 8, at % 8
        for other in range(8):
            for k in range(2):
                team, slot = place_of_unit(2 * (8 * half + other) + k)
                table[at, 12 + 2 * other + k] = slot if team == member else 0
        for k in range(2):
            table[at, 28 + k] = place_of_unit(2 * at + k)[0]
    return table


def device_info():
    at = lax.axis_index(UNIT_AXES).astype(jnp.uint32)
    return lax.dynamic_slice(jnp.asarray(device_table()), (at, jnp.uint32(0)), (1, 30)).reshape(30)


def pick_units_kernel(info, w, *outs):
    for r, out in enumerate(outs):
        out[...] = w[info[4 + r]]


def place_units_kernel(info, g0, g1, g2, g3, out):
    for r, got in enumerate((g0, g1, g2, g3)):
        out[info[8 + r]] = got[...]


def send_early_kernel(info, half, more, out):
    for member in range(TEAM):
        out[member, :UP_TILES] = half[member * UP_TILES : (member + 1) * UP_TILES]
        for k in range(2):
            at = UP_TILES + 8 * k
            out[member, at : at + 8] = more[info[12 + 2 * member + k]]


def got_early_kernel(info, got, half, out):
    for member in range(TEAM):
        out[member * UP_TILES : (member + 1) * UP_TILES] = got[member, :UP_TILES]
    at = TEAM * UP_TILES
    out[at : at + DOWN_TILES] = half[at : at + DOWN_TILES]
    for k in range(2):
        first = at + DOWN_TILES + 8 * k
        out[first : first + 8] = got[info[28 + k], UP_TILES + 8 * k : UP_TILES + 8 * (k + 1)]


def spread_units(w, info):
    pieces = call(pick_units_kernel, [(w.shape[1:], bf)] * 4, [], info, w)
    got = [
        lax.ppermute(piece, UNIT_AXES, [(e[0], e[1]) for e in route])
        for piece, route in zip(pieces, ROUTES)
    ]
    return call(place_units_kernel, [((4, *w.shape[1:]), bf)], [], info, *got)[0]


def pack_layout(lengths_row, count_of_blocks, rows_per_block):
    used_blocks = (lengths_row + rows_per_block - 1) // rows_per_block
    first_block = jnp.cumsum(used_blocks) - used_blocks
    block_order = jnp.arange(count_of_blocks, dtype=jnp.int32)
    covers = (
        (block_order[:, None] >= first_block[None, :])
        & (block_order[:, None] < (first_block + used_blocks)[None, :])
    ).astype(jnp.int32)
    occupied = jnp.sum(covers, axis=1) > 0
    slot_order = jnp.arange(lengths_row.shape[0], dtype=jnp.int32)
    segment = jnp.where(occupied, jnp.sum(covers * slot_order[None, :], axis=1), -1)
    begins = jnp.sum(covers * first_block[None, :], axis=1)
    seq_length = jnp.sum(covers * lengths_row[None, :], axis=1)
    within = (block_order - begins)[:, None] * rows_per_block + jnp.arange(
        rows_per_block, dtype=jnp.int32
    )[None, :]
    is_valid = occupied[:, None] & (within < seq_length[:, None])
    carry_flag = occupied & (block_order > begins)
    return (segment, within, is_valid, carry_flag)


def facts(lengths_row, half, team):
    segment, within, is_valid, carry = pack_layout(lengths_row, 2 * TEAM, BLOCK)
    start = half * SEQ

    def mine(x):
        return lax.dynamic_slice_in_dim(x, start, SEQ, 0)

    seg_rows = jnp.repeat(segment, BLOCK)
    chain = jnp.cumsum(1 - carry.astype(jnp.int32))
    chain_rows = mine(jnp.repeat(chain, BLOCK))
    carry_rows = mine(jnp.repeat(carry, BLOCK)).astype(f32)
    position = mine(within.reshape(-1))
    valid = is_valid.reshape(-1)
    own_valid = lax.dynamic_slice_in_dim(valid, start + team * BLOCK, BLOCK, 0)
    half_width = HEAD_SIZE // 2
    frequency = rope_base ** (-jnp.arange(half_width, dtype=f32) / half_width)
    angles = position.astype(f32)[:, None] * frequency[None, :]
    cos, sin = jnp.cos(angles), jnp.sin(angles)
    enters = ((chain_rows == chain_rows[0]) & (carry_rows[0] > 0)).astype(f32)
    leaves = (chain_rows == chain_rows[SEQ - 1]).astype(f32)
    key_seg = jnp.where(valid, seg_rows, -2).astype(f32)
    columns = [mine(seg_rows).astype(f32), chain_rows.astype(f32), enters, leaves, carry_rows]
    rows = [mine(key_seg), jnp.where(half == 1, key_seg[:SEQ], -3.0), chain_rows.astype(f32)]
    return dict(
        trig=jnp.concatenate([cos, cos, cos, cos, -sin, sin, -sin, sin], axis=1),
        valid=own_valid.astype(f32)[:, None],
        rowf=jnp.pad(jnp.stack(columns, axis=1), ((0, 0), (0, 128 - len(columns)))),
        colf=jnp.pad(jnp.stack(rows), ((0, 8 - len(rows)), (0, 0))),
        info=device_info(),
        half=half,
    )


def norm(x, gain):
    r = lax.rsqrt(jnp.mean(x * x, axis=-1, keepdims=True) + norm_epsilon)
    return x * r * gain, r


def norm_back(grad, x, r, gain):
    e = grad * gain
    gx = r * e - x * (r * r * r) * jnp.mean(x * e, axis=-1, keepdims=True)
    return gx


def half_first(x):
    middle = x.shape[1] // 2
    turned = jnp.concatenate([x[:, middle:], x[:, :middle]], axis=1)
    return jnp.where(lax.axis_index("zhi") == 0, x, turned)


def to_first(x):
    return lax.ppermute(x, "zhi", [(1, 0)])


ROWS = 128
STEPS = SEQ // ROWS
B_AT, C_AT, X_AT, Z_AT, Q_AT, V_AT = 0, 128, 256, 448, 640, 768
PACKED = SEQ + CH + 64
PAD = 16
LANE = 64


def nt(left, right):
    return lax.dot_general(left, right, (((1,), (1,)), ((), ())), preferred_element_type=f32)


def tn(left, right):
    return lax.dot_general(left, right, (((0,), (0,)), ((), ())), preferred_element_type=f32)


def exact(left, right):
    return jnp.dot(left, right, precision=lax.Precision.HIGHEST, preferred_element_type=f32)


def iota(shape, axis):
    return lax.broadcasted_iota(jnp.int32, shape, axis)


def head(x, k):
    return x[:, k * HEAD_SIZE : (k + 1) * HEAD_SIZE]


def lane(x, k):
    return x[:, LANE + k : LANE + k + 1]


def on_lanes(columns):
    at = iota((columns[0].shape[0], 128), 1)
    total = jnp.zeros((columns[0].shape[0], 128), f32)
    for k, column in enumerate(columns):
        total = jnp.where(at == LANE + k, column, total)
    return total


def assemble(info, pieces, others, rows):
    y, core = info[0], info[1]
    for back in range(4):
        at = ((y - back) & 3) * ROWS
        rows[pl.ds(pl.multiple_of(at + core * BLOCK, BLOCK), BLOCK), :] = pieces[back][...]
        rows[pl.ds(pl.multiple_of(at + (1 - core) * BLOCK, BLOCK), BLOCK), :] = others[back]


def deliver(info, value, step, mine, other):
    first = info[1] == 0
    to = (step - info[0]) & 3
    upper, lower = value[:BLOCK].astype(bf), value[BLOCK:].astype(bf)
    mine[to] = jnp.where(first, upper, lower)
    other[to] = jnp.where(first, lower, upper)


def swapped_halves(x):
    q = HEAD_SIZE // 2
    return jnp.concatenate([x[:, q : 2 * q], x[:, :q], x[:, 3 * q :], x[:, 2 * q : 3 * q]], axis=1)


def tap_mask(rowf, at, tap):
    within = iota((ROWS, 1), 0) & (BLOCK - 1)
    return jnp.where(within + tap >= KC - 1, 1.0, rowf[at : at + ROWS, 4:5])


def tap_rows(pad, rowf, at, tap):
    first = PAD - (KC - 1) + tap + at
    return pad[first : first + ROWS, :] * tap_mask(rowf, at, tap)


def conv_pre(pad, rowf, cw, at):
    pre = cw[4:5, :]
    for tap in range(KC):
        pre = pre + cw[tap : tap + 1, :] * tap_rows(pad, rowf, at, tap)
    return pre


def fill_pad(pad, mixed, edge):
    if edge is None:
        pad[:PAD, :] = jnp.zeros((PAD, CONV), f32)
    else:
        at = SEQ + CH
        whole = jnp.concatenate([edge[at + 16 * k : at + 16 * (k + 1), :] for k in range(4)], axis=1)
        pad[:PAD, :] = whole[:, :CONV].astype(f32)
    for at in range(0, SEQ, ROWS):
        pad[PAD + at : PAD + at + ROWS, :] = mixed[at : at + ROWS, :CONV].astype(bf).astype(f32)


def write_edge(out, rows):
    at = SEQ + CH
    for k in range(4):
        out[at + 16 * k : at + 16 * (k + 1), :] = rows[:, 128 * k : 128 * (k + 1)].astype(bf)


def mix_kernel(
    info, p0, p1, p2, p3, others, gains, wm, trig, rowf, cw, hv, rows, mixed, cs, qkv, pack, pad, raw
):
    assemble(info, (p0, p1, p2, p3), others, raw)
    middle = raw.shape[1] // 2
    lower = (iota((ROWS, ROWS), 0) >= iota((ROWS, ROWS), 1)).astype(f32)
    base = jnp.zeros((1, 128), f32)
    low_lanes = iota((ROWS, 128), 1) < HEAD_SIZE
    for at in range(0, SEQ, ROWS):
        r = slice(at, at + ROWS)
        x = raw[r, :].astype(f32)
        root = lax.rsqrt(jnp.mean(x * x, axis=1, keepdims=True) + norm_epsilon)
        n = (x * root * gains[0:1, :]).astype(bf)
        turned = jnp.concatenate([n[:, middle:], n[:, :middle]], axis=1)
        n = jnp.where(info[2] == 0, n, turned)
        rows[r, :] = n
        m = jnp.dot(n, wm[...], preferred_element_type=f32)
        mixed[r, :] = m
        qk = m[:, Q_AT:V_AT]
        qk = qk * trig[r, :128] + swapped_halves(qk) * trig[r, 128:]
        last = m[:, V_AT:]
        qkv[r, :128] = qk.astype(bf)
        qkv[r, 128:] = last.astype(bf)
        pack[r, :] = jnp.where(low_lanes, last, qk).astype(bf)
        step = jax.nn.softplus(last + hv[0:1, :])
        cum = exact(lower, step * hv[1:2, :]) + base
        base = cum[ROWS - 1 :, :]
        cs[r, :128] = cum
        cs[r, 128:] = step
    fill_pad(pad, mixed, None)
    state = jnp.zeros((CH, STATE_SIZE), f32)
    for at in range(0, SEQ, ROWS):
        r = slice(at, at + ROWS)
        act = jax.nn.silu(conv_pre(pad, rowf, cw, at))
        scale = jnp.exp(base - cs[r, :128]) * cs[r, 128:] * rowf[r, 3:4]
        scaled = jnp.concatenate(
            [head(act[:, X_AT:], k) * lane(scale, k) for k in range(HEADS)], axis=1
        )
        state = state + tn(scaled.astype(bf), act[:, B_AT:C_AT].astype(bf))
    pack[SEQ : SEQ + CH, :] = state.astype(bf)
    write_edge(pack, mixed[SEQ - 16 :, :512])


def own_scores(qkv, colf, rowf, at):
    n = at + ROWS
    s = nt(qkv[at:n, :HEAD_SIZE], qkv[:n, HEAD_SIZE : 2 * HEAD_SIZE]) * HEAD_SIZE**-0.5
    row, col = at + iota((ROWS, n), 0), iota((ROWS, n), 1)
    ok = ((rowf[at:n, 0:1] == colf[0:1, :n]) & (col <= row)) | (col == row)
    return jnp.where(ok, s, masked_score)


def other_scores(qkv, got, colf, rowf, at):
    r = slice(at, at + ROWS)
    s = nt(qkv[r, :HEAD_SIZE], got[:SEQ, HEAD_SIZE:]) * HEAD_SIZE**-0.5
    return jnp.where(rowf[r, 0:1] == colf[1:2, :], s, masked_score)


def decay_of(cs, cum_t, linked, at, k):
    n = at + ROWS
    gap = cs[at:n, LANE + k : LANE + k + 1] - cum_t[LANE + k : LANE + k + 1, :n]
    return jnp.where(linked, jnp.exp(jnp.minimum(gap, 0.0)), 0.0)


def linked_rows(rowf, colf, at):
    n = at + ROWS
    row, col = at + iota((ROWS, n), 0), iota((ROWS, n), 1)
    return (rowf[at:n, 1:2] == colf[2:3, :n]) & (col <= row)


def head_kernel(
    info, mixed, cs, qkv, got, wout, rowf, colf, cw, hv, mine, other, joined, ssm_out, stats,
    pad, act, cum_t, step_t,
):
    fill_pad(pad, mixed, got)
    cum_t[...] = cs[:, :128].T
    step_t[...] = cs[:, 128:].T
    for at in range(0, SEQ, ROWS):
        r, n = slice(at, at + ROWS), at + ROWS
        own = own_scores(qkv, colf, rowf, at)
        far = other_scores(qkv, got, colf, rowf, at)
        peak = jnp.maximum(
            jnp.max(own, axis=1, keepdims=True), jnp.max(far, axis=1, keepdims=True)
        )
        own, far = jnp.exp(own - peak), jnp.exp(far - peak)
        total = jnp.sum(own, axis=1, keepdims=True) + jnp.sum(far, axis=1, keepdims=True)
        stats[r, :] = jnp.broadcast_to(peak + jnp.log(total), (ROWS, 128))
        scale = 1.0 / total
        attended = mm((own * scale).astype(bf), qkv[:n, 128 : 128 + HEAD_SIZE]) + mm(
            (far * scale).astype(bf), got[:SEQ, :HEAD_SIZE]
        )
        a = jax.nn.silu(conv_pre(pad, rowf, cw, at))
        act[r, :] = a.astype(bf)
        c_low = act[r, C_AT:X_AT]
        meet = nt(c_low, act[:n, B_AT:C_AT])
        linked = linked_rows(rowf, colf, at)
        carried = nt(c_low, got[SEQ : SEQ + CH, :])
        in_scale = jnp.exp(cs[r, :128]) * rowf[r, 2:3]
        outs = []
        for k in range(HEADS):
            weights = meet * decay_of(cs, cum_t, linked, at, k) * step_t[LANE + k : LANE + k + 1, :n]
            x_at = X_AT + k * HEAD_SIZE
            outs.append(
                mm(weights.astype(bf), act[:n, x_at : x_at + HEAD_SIZE])
                + lane(in_scale, k) * head(carried, k)
                + hv[2:3, LANE + k : LANE + k + 1] * head(a[:, X_AT:], k)
            )
        ssm = jnp.concatenate(outs, axis=1)
        ssm_out[r, :] = ssm
        j = jnp.concatenate([attended, ssm * jax.nn.silu(mixed[r, Z_AT:Q_AT])], axis=1).astype(bf)
        joined[r, :] = j
        deliver(info, mm(j, wout[...]), at // ROWS, mine, other)


def ffn_kernel(info, p0, p1, p2, p3, others, wup, wdown, rows, gate_up, hidden, mine, other):
    assemble(info, (p0, p1, p2, p3), others, rows)
    for at in range(0, SEQ, ROWS):
        r = slice(at, at + ROWS)
        gu = mm(rows[r, :], wup[...])
        gate_up[r, :] = gu
        h = (jax.nn.silu(gu[:, :HID]) * gu[:, HID:]).astype(bf)
        hidden[r, :] = h
        deliver(info, mm(h, wdown[...]), at // ROWS, mine, other)


def slope(z):
    s = jax.nn.sigmoid(z)
    return s * (1.0 + z * (1.0 - s))


def half_order(info, row):
    middle = row.shape[1] // 2
    turned = jnp.concatenate([row[:, middle:], row[:, :middle]], axis=1)
    return jnp.where(info[2] == 0, row, turned)


def ffn_back_kernel(
    info, p0, p1, p2, p3, others, wup, wdown, gate_up, normed, gains,
    rows, grad_up, mine, other, g_gain,
):
    assemble(info, (p0, p1, p2, p3), others, rows)
    total = jnp.zeros((1, rows.shape[1]), f32)
    for at in range(0, SEQ, ROWS):
        r = slice(at, at + ROWS)
        gh = nt(rows[r, :], wdown[...])
        gate, up = gate_up[r, :HID], gate_up[r, HID:]
        g = jnp.concatenate([gh * up * slope(gate), gh * jax.nn.silu(gate)], axis=1).astype(bf)
        grad_up[r, :] = g
        back = nt(g, wup[...])
        total = total + jnp.sum(back * normed[r, :].astype(f32), axis=0, keepdims=True)
        deliver(info, back, at // ROWS, mine, other)
    g_gain[...] = jnp.broadcast_to(total / half_order(info, gains[1:2, :]), g_gain.shape)


def head_back_kernel(
    info, p0, p1, p2, p3, others, wout, mixed, cs, qkv, got, ssm, stats, rowf, colf, cw, hv,
    rows, g_act, g_cs, g_qkv, g_z, send, g_skip,
    pad, act, cum_t, step_t, own_t, far_t, act_t, column,
):
    assemble(info, (p0, p1, p2, p3), others, rows)
    fill_pad(pad, mixed, got)
    cum_t[...] = cs[:, :128].T
    step_t[...] = cs[:, 128:].T
    own_t[...] = jnp.zeros((128, SEQ), f32)
    far_t[...] = jnp.zeros((128, SEQ), f32)
    act_t[...] = jnp.zeros((128 + CH, SEQ), f32)
    column[...] = jnp.zeros((128, SEQ), f32)
    state_t = jnp.zeros((STATE_SIZE, CH), f32)
    skips = [jnp.zeros((1, 1), f32) for _ in range(HEADS)]
    for at in range(0, SEQ, ROWS):
        r, n = slice(at, at + ROWS), at + ROWS
        a = jax.nn.silu(conv_pre(pad, rowf, cw, at))
        act[r, :] = a.astype(bf)
        gj = nt(rows[r, :], wout[...])
        g_att = gj[:, :HEAD_SIZE].astype(bf)
        gated = gj[:, HEAD_SIZE:]
        z = mixed[r, Z_AT:Q_AT]
        g_ssm = gated * jax.nn.silu(z)
        g_z[r, :] = gated * ssm[r, :] * slope(z)
        lse = stats[r, 0:1]
        p_own = jnp.exp(own_scores(qkv, colf, rowf, at) - lse)
        p_far = jnp.exp(other_scores(qkv, got, colf, rowf, at) - lse)
        g_own = nt(g_att, qkv[:n, 128 : 128 + HEAD_SIZE])
        g_far = nt(g_att, got[:SEQ, :HEAD_SIZE])
        total = jnp.sum(p_own * g_own, axis=1, keepdims=True) + jnp.sum(
            p_far * g_far, axis=1, keepdims=True
        )
        s_own = (p_own * (g_own - total) * HEAD_SIZE**-0.5).astype(bf)
        s_far = (p_far * (g_far - total) * HEAD_SIZE**-0.5).astype(bf)
        query = qkv[r, :HEAD_SIZE].astype(f32)
        g_qkv[r, :HEAD_SIZE] = mm(s_own, qkv[:n, HEAD_SIZE : 2 * HEAD_SIZE]) + mm(
            s_far, got[:SEQ, HEAD_SIZE:]
        )
        turned = jnp.concatenate([gj[:, :HEAD_SIZE], query], axis=1).T.astype(bf)
        att_t, query_t = turned[:HEAD_SIZE], turned[HEAD_SIZE:]
        own_t[:HEAD_SIZE, :n] += mm(att_t, p_own.astype(bf))
        own_t[HEAD_SIZE:, :n] += mm(query_t, s_own)
        far_t[:HEAD_SIZE, :] += mm(att_t, p_far.astype(bf))
        far_t[HEAD_SIZE:, :] += mm(query_t, s_far)
        c_low = act[r, C_AT:X_AT]
        meet = nt(c_low, act[:n, B_AT:C_AT])
        linked = linked_rows(rowf, colf, at)
        state = got[SEQ : SEQ + CH, :]
        carried = nt(c_low, state)
        in_scale = jnp.exp(cs[r, :128]) * rowf[r, 2:3]
        g_meet = jnp.zeros((ROWS, n), f32)
        g_carried, g_cum = [], []
        turned = jnp.concatenate([a[:, C_AT:X_AT], g_ssm, jnp.zeros((ROWS, 64), f32)], axis=1)
        turned = turned.T.astype(bf)
        c_t = turned[:STATE_SIZE]
        for k in range(HEADS):
            x_at = X_AT + k * HEAD_SIZE
            xk, gk = head(a[:, X_AT:], k), head(g_ssm, k)
            g_low = gk.astype(bf)
            decay = decay_of(cs, cum_t, linked, at, k)
            step_row = step_t[LANE + k : LANE + k + 1, :n]
            part = nt(g_low, act[:n, x_at : x_at + HEAD_SIZE]) * decay
            g_meet = g_meet + part * step_row
            product = part * meet
            column[LANE + k : LANE + k + 1, :n] += jnp.sum(product, axis=0, keepdims=True)
            row = jnp.sum(product * step_row, axis=1, keepdims=True)
            t_at = 128 + k * HEAD_SIZE
            act_t[t_at : t_at + HEAD_SIZE, :n] += mm(
                turned[t_at : t_at + HEAD_SIZE], (meet * decay * step_row).astype(bf)
            )
            g_act[r, x_at : x_at + HEAD_SIZE] = hv[2:3, LANE + k : LANE + k + 1] * gk
            g_scale = jnp.sum(gk * head(carried, k), axis=1, keepdims=True)
            g_cum.append(row + g_scale * lane(in_scale, k))
            g_carried.append(gk * lane(in_scale, k))
            skips[k] = skips[k] + jnp.sum(
                jnp.sum(gk * xk, axis=1, keepdims=True), axis=0, keepdims=True
            )
        g_cs[r, :128] = on_lanes(g_cum)
        g_carried = jnp.concatenate(g_carried, axis=1).astype(bf)
        g_meet = g_meet.astype(bf)
        g_act[r, C_AT:X_AT] = mm(g_meet, act[:n, B_AT:C_AT]) + mm(g_carried, state)
        act_t[:STATE_SIZE, :n] += mm(c_t, g_meet)
        state_t = state_t + mm(c_t, g_carried)
    g_act[:, B_AT:C_AT] = act_t[:STATE_SIZE, :].T
    g_act[:, X_AT:] += act_t[STATE_SIZE:, :].T
    own_kv = own_t[...].T
    g_qkv[:, HEAD_SIZE : 2 * HEAD_SIZE] = own_kv[:, HEAD_SIZE:]
    g_qkv[:, 128 : 128 + HEAD_SIZE] = own_kv[:, :HEAD_SIZE]
    g_qkv[:, 128 + HEAD_SIZE :] = jnp.zeros((SEQ, HEAD_SIZE), f32)
    turned = column[...].T
    g_cs[:, :128] = g_cs[:, :128] - turned * cs[:, 128:]
    g_cs[:, 128:] = turned
    g_skip[...] = jnp.broadcast_to(on_lanes(skips), (8, 128))
    send[:SEQ, :] = far_t[...].T.astype(bf)
    send[SEQ : SEQ + CH, :] = state_t.T.astype(bf)
    edge = g_act[:PAD, :] * slope(conv_pre(pad, rowf, cw, 0)[:PAD])
    pad[:PAD, :] = jnp.zeros((PAD, CONV), f32)
    for tap in range(KC - 1):
        first = PAD - (KC - 1) + tap
        count = PAD - first
        pad[first:PAD, :] += (
            cw[tap : tap + 1, :] * tap_mask(rowf, 0, tap)[:count] * edge[:count]
        )
    write_edge(send, jnp.concatenate([pad[:PAD, :], jnp.zeros((PAD, 64), f32)], axis=1))


def mix_back_kernel(
    info, mixed, cs, got, g_act, g_cs, g_qkv, g_z, g_skip, back, wm, trig, rowf, cw, hv,
    normed, gains, gain_two, grad, mine, other, small, pad, g_pad, acc,
):
    fill_pad(pad, mixed, got)
    total = cs[SEQ - 1 :, :128]
    state = back[SEQ : SEQ + CH, :]
    shift = jnp.zeros((1, 128), f32)
    g_pad[...] = jnp.zeros((PAD + SEQ, CONV), f32)
    kernels = [jnp.zeros((1, CONV), f32) for _ in range(KC + 1)]
    for at in range(0, SEQ, ROWS):
        r = slice(at, at + ROWS)
        pre = conv_pre(pad, rowf, cw, at)
        a = jax.nn.silu(pre)
        pulled = nt(a[:, B_AT:C_AT].astype(bf), state)
        tail = jnp.exp(total - cs[r, :128]) * rowf[r, 3:4]
        scale = tail * cs[r, 128:]
        scaled, g_x, g_scale = [], [], []
        for k in range(HEADS):
            xk, pk = head(a[:, X_AT:], k), head(pulled, k)
            g_scale.append(jnp.sum(xk * pk, axis=1, keepdims=True))
            g_x.append(pk * lane(scale, k))
            scaled.append(xk * lane(scale, k))
        g_scale = on_lanes(g_scale)
        change = g_scale * scale
        shift = shift + jnp.sum(change, axis=0, keepdims=True)
        acc[r, :128] = g_cs[r, :128] - change
        acc[r, 128:] = g_cs[r, 128:] + g_scale * tail
        g_b = mm(jnp.concatenate(scaled, axis=1).astype(bf), state)
        more = jnp.concatenate([g_b, jnp.zeros((ROWS, 128), f32), *g_x], axis=1)
        g_pre = (g_act[r, :] + more) * slope(pre)
        kernels[KC] = kernels[KC] + jnp.sum(g_pre, axis=0, keepdims=True)
        for tap in range(KC):
            kernels[tap] = kernels[tap] + jnp.sum(
                g_pre * tap_rows(pad, rowf, at, tap), axis=0, keepdims=True
            )
            first = PAD - (KC - 1) + tap + at
            g_pad[first : first + ROWS, :] += (
                cw[tap : tap + 1, :] * tap_mask(rowf, at, tap) * g_pre
            )
    edge_at = SEQ + CH
    edge = jnp.concatenate(
        [back[edge_at + 16 * k : edge_at + 16 * (k + 1), :] for k in range(4)], axis=1
    )
    g_pad[SEQ:, :] += edge[:, :CONV].astype(f32)
    upper = (iota((ROWS, ROWS), 0) <= iota((ROWS, ROWS), 1)).astype(f32)
    lanes = iota((ROWS, 128), 1)
    on_step = (lanes >= LANE) & (lanes < LANE + HEADS)
    g_bias, g_rate = jnp.zeros((1, 128), f32), jnp.zeros((1, 128), f32)
    g_gain = jnp.zeros((1, normed.shape[1]), f32)
    for at in reversed(range(0, SEQ, ROWS)):
        r = slice(at, at + ROWS)
        later = exact(upper, acc[r, :128]) + shift
        shift = later[:1, :]
        rate = hv[1:2, :]
        g_rate = g_rate + jnp.sum(later * cs[r, 128:] * rate, axis=0, keepdims=True)
        g_raw = (acc[r, 128:] + later * rate) * jax.nn.sigmoid(mixed[r, V_AT:] + hv[0:1, :])
        g_raw = jnp.where(on_step, g_raw, 0.0)
        g_bias = g_bias + jnp.sum(g_raw, axis=0, keepdims=True)
        arrived = back[r, :].astype(f32)
        qk = g_qkv[r, :128] + jnp.where(lanes >= HEAD_SIZE, arrived, 0.0)
        qk = qk * trig[r, :128] - swapped_halves(qk) * trig[r, 128:]
        last = jnp.where(lanes < HEAD_SIZE, g_qkv[r, 128:] + arrived, g_raw)
        g = jnp.concatenate([g_pad[PAD + at : PAD + at + ROWS, :], g_z[r, :], qk, last], axis=1)
        g = g.astype(bf)
        grad[r, :] = g
        g_rows = nt(g, wm[...])
        g_gain = g_gain + jnp.sum(g_rows * normed[r, :].astype(f32), axis=0, keepdims=True)
        deliver(info, g_rows, at // ROWS, mine, other)
    g_gain = g_gain / half_order(info, gains[0:1, :])
    fill = jnp.zeros((1, 64), f32)
    none = jnp.zeros((1, 128), f32)
    conv = [jnp.concatenate([k, fill], axis=1) for k in kernels]
    chunks = [
        jnp.concatenate([c[:, 128 * k : 128 * k + 128] for c in conv], axis=0) for k in range(4)
    ]
    for q in range(2):
        tile = jnp.concatenate([chunks[2 * q], chunks[2 * q + 1], *[none] * 6], axis=0).astype(bf)
        for owner in range(2 * TEAM):
            small[1 + q, owner] = tile
    heads = jnp.concatenate([g_bias, g_rate, g_skip[:1, :], *[none] * 11], axis=0)
    for owner in range(2 * TEAM):
        at = (owner % TEAM) * BLOCK + (SEQ if owner < TEAM else 0)
        own = [
            jnp.concatenate([row[:, at : at + BLOCK], fill], axis=1)
            for row in (g_gain, gain_two[:1, :])
        ]
        small[0, owner] = jnp.concatenate([*own, heads], axis=0).astype(bf)
        small[3, owner] = jnp.zeros((16, 128), bf)


UP_TILES = 2 * HID // 128
MIX_TILES = COLS // 128
DOWN_TILES = 16
EARLY = TEAM * UP_TILES + DOWN_TILES
LATE = TEAM * MIX_TILES
OUT_TILES = 32


def put_rows(out, block, at, tiles, half_tiles):
    base = half_tiles if at < SEQ else 0
    for q in range(8):
        member = (at % SEQ) // BLOCK + q // 4
        for c in range(tiles):
            tile = block[16 * q : 16 * q + 16, 128 * c : 128 * c + 128]
            out[q % 4, base + member * tiles + c] = tile


def early_kernel(info, rows_two, grad_up, hidden, grad_rows, joined, branch, out):
    width = rows_two.shape[1]
    for at in range(0, width, 128):
        block = tn(rows_two[:, at : at + 128], grad_up[...]).astype(bf)
        put_rows(out, block, at, UP_TILES, EARLY)
    for part in range(2):
        base = jnp.where(info[2] == part, EARLY, 0) + TEAM * UP_TILES
        block = tn(hidden[:, 128 * part : 128 * part + 128], grad_rows[...]).astype(bf)
        for q in range(8):
            for c in range(8):
                tile = block[16 * q : 16 * q + 16, 128 * c : 128 * c + 128]
                out[q // 2, base + (q % 2) * 8 + c] = tile
        block = tn(joined[:, 128 * part : 128 * part + 128], branch[...]).astype(bf)
        for q in range(8):
            for c in range(8):
                tile = block[16 * q : 16 * q + 16, 128 * c : 128 * c + 128]
                out[q % 4, 2 * EARLY + (2 * part + q // 4) * 8 + c] = tile


def late_kernel(info, rows, grad, small, out):
    for q in range(4):
        for half in range(2):
            at = half * (LATE + TEAM) + LATE
            out[q, at : at + TEAM] = small[q, half * TEAM : (half + 1) * TEAM]
    for at in range(0, rows.shape[1], 128):
        block = tn(rows[:, at : at + 128], grad[...]).astype(bf)
        put_rows(out, block, at, MIX_TILES, LATE + TEAM)


def call(kernel, outs, scratch, *args, ties=()):
    ties = jax.tree.leaves(ties)
    specs = [pl.BlockSpec(memory_space=pltpu.SMEM)]
    specs += [pl.BlockSpec(memory_space=pltpu.VMEM)] * (len(args) - 1)
    specs += [pl.BlockSpec(memory_space=pl.ANY)] * len(ties)
    first, last = len(args), len(args) + len(ties)

    def body(*refs):
        kernel(*refs[:first], *refs[last:])

    return pl.pallas_call(
        body,
        out_shape=[jax.ShapeDtypeStruct(s, t) for s, t in outs],
        in_specs=specs,
        out_specs=[pl.BlockSpec(memory_space=pltpu.VMEM)] * len(outs),
        scratch_shapes=[pltpu.VMEM(s, t) for s, t in scratch],
        compiler_params=pltpu.CompilerParams(vmem_limit_bytes=20 * 1024 * 1024),
    )(*args, *ties)


TO_TEAM = [((4, BLOCK, 1024), bf), ((4, BLOCK, 1024), bf)]
CONV_PAD = ((PAD + SEQ, CONV), f32)


def gather_team(x):
    pieces = [x] + [shifted(x, "y", by, 4) for by in (1, 2, 3)]
    return (*pieces, swap(jnp.stack(pieces), "core"))


def sum_team(mine, other):
    pair = mine.astype(f32) + swap(other, "core").astype(f32)
    total = pair[0]
    for by in (1, 2, 3):
        total = total + shifted(pair[by].astype(bf), "y", by, 4).astype(f32)
    return total


def layer_forward(w, x_low, lay, team, before=()):
    info, rowf, colf, trig = lay["info"], lay["rowf"], lay["colf"], lay["trig"]
    x = x_low.astype(f32)
    rows, mixed, cs, qkv, pack = call(
        mix_kernel,
        [((SEQ, 1024), bf), ((SEQ, COLS), f32), ((SEQ, 256), f32), ((SEQ, 256), bf), ((PACKED, 128), bf)],
        [CONV_PAD, ((SEQ, 1024), bf)],
        info, *team, w["gains"], w["mix"], trig, rowf, w["cw"], w["hv"],
    )
    got = after(swap(pack, "zhi"), before)
    keep = jnp.where((jnp.arange(PACKED) < SEQ) | (lay["half"] == 1), 1.0, 0.0).astype(bf)
    got = got * keep[:, None]
    mine, other, joined, ssm, stats = call(
        head_kernel,
        [*TO_TEAM, ((SEQ, 256), bf), ((SEQ, CH), f32), ((SEQ, 128), f32)],
        [CONV_PAD, ((SEQ, CONV), bf), ((128, SEQ), f32), ((128, SEQ), f32)],
        info, mixed, cs, qkv, got, w["out"], rowf, colf, w["cw"], w["hv"],
    )
    resid = x + sum_team(mine, other)
    normed_two, r2 = norm(resid, w["gains"][1])
    team = gather_team(half_first(normed_two.astype(bf)))
    rows_two, gate_up, hidden, mine, other = call(
        ffn_kernel,
        [((SEQ, 1024), bf), ((SEQ, 2 * HID), f32), ((SEQ, HID), bf), *TO_TEAM],
        [],
        info, *team, w["gate_up"], w["down"],
    )
    kept = dict(
        x=x, rows=rows, mixed=mixed, cs=cs, qkv=qkv, got=got, joined=joined, ssm=ssm, stats=stats,
        resid=resid, r2=r2, rows_two=rows_two, gate_up=gate_up, hidden=hidden,
    )
    return (mine, other), kept


def layer_output(parts, kept, lay):
    return (lay["valid"] * (kept["resid"] + sum_team(*parts))).astype(bf)


def layer_backward(w, kept, grad, lay, team, before=(), earlier=((), ())):
    info, rowf, colf, trig = lay["info"], lay["rowf"], lay["colf"], lay["trig"]
    grad_rows, grad_up, mine, other, gain_two = call(
        ffn_back_kernel,
        [((SEQ, 1024), bf), ((SEQ, 2 * HID), bf), *TO_TEAM, ((8, 1024), f32)],
        [],
        info, *team, w["gate_up"], w["down"], kept["gate_up"], kept["rows_two"], w["gains"],
    )
    back = half_first(sum_team(mine, other))
    gx = norm_back(back, kept["resid"], kept["r2"], w["gains"][1])
    grad_resid = grad + gx
    team = gather_team(grad_resid.astype(bf))
    branch_rows, g_act, g_cs, g_qkv, g_z, send, g_skip = call(
        head_back_kernel,
        [((SEQ, 1024), bf), ((SEQ, CONV), f32), ((SEQ, 256), f32), ((SEQ, 256), f32), ((SEQ, CH), f32),
         ((PACKED, 128), bf), ((8, 128), f32)],
        [CONV_PAD, ((SEQ, CONV), bf), ((128, SEQ), f32), ((128, SEQ), f32), ((128, SEQ), f32),
         ((128, SEQ), f32), ((128 + CH, SEQ), f32), ((128, SEQ), f32)],
        info, *team, w["out"], kept["mixed"], kept["cs"], kept["qkv"], kept["got"], kept["ssm"],
        kept["stats"], rowf, colf, w["cw"], w["hv"],
    )
    early = call(
        early_kernel,
        [((4, 2 * EARLY + OUT_TILES, 16, 128), bf)],
        [],
        info, kept["rows_two"], grad_up, kept["hidden"], grad_rows, kept["joined"], branch_rows,
    )[0]
    arrived = to_first(send)
    early_rows = early
    early = lax.psum_scatter(early, "rep", scatter_dimension=0, tiled=False)
    grad_mixed, mine, other, small = call(
        mix_back_kernel,
        [((SEQ, COLS), bf), *TO_TEAM, ((4, 2 * TEAM, 16, 128), bf)],
        [CONV_PAD, CONV_PAD, ((SEQ, 256), f32)],
        info, kept["mixed"], kept["cs"], kept["got"], g_act, g_cs, g_qkv, g_z, g_skip, arrived,
        w["mix"], trig, rowf, w["cw"], w["hv"], kept["rows"], w["gains"], gain_two,
        ties=(early_rows, before, earlier),
    )
    late = call(
        late_kernel,
        [((4, 2 * (LATE + TEAM), 16, 128), bf)],
        [],
        info, kept["rows"], grad_mixed, small,
    )[0]
    back = half_first(sum_team(mine, other))
    late = lax.psum_scatter(late, "rep", scatter_dimension=0, tiled=False)
    r1 = lax.rsqrt(jnp.mean(kept["x"] * kept["x"], axis=-1, keepdims=True) + norm_epsilon)
    gx = norm_back(back, kept["x"], r1, w["gains"][0])
    grads = dict(early=early, late=late)
    return grad_resid + gx, grads


SMALL = 768


def team_columns(w_mix, w_step):
    rows = w_mix.shape[0]
    at = SPACE_CHANNELS + SPACE_CHANNELS
    state = w_mix[:, at : at + 2 * STATE_SIZE]
    at += 2 * STATE_SIZE
    query = w_mix[:, at : at + QUERY_HEADS * HEAD_SIZE].reshape(rows, TEAM, HEAD_SIZE)
    at += QUERY_HEADS * HEAD_SIZE
    key = w_mix[:, at : at + 2 * HEAD_SIZE].reshape(rows, 2, HEAD_SIZE)
    value = w_mix[:, at + 2 * HEAD_SIZE :].reshape(rows, 2, HEAD_SIZE)
    pieces = [
        jnp.broadcast_to(state[:, None], (rows, TEAM, 2 * STATE_SIZE)),
        w_mix[:, SPACE_CHANNELS : 2 * SPACE_CHANNELS].reshape(rows, TEAM, CH),
        w_mix[:, :SPACE_CHANNELS].reshape(rows, TEAM, CH),
        query,
        jnp.repeat(key, TEAM // 2, axis=1),
        jnp.repeat(value, TEAM // 2, axis=1),
        w_step.reshape(rows, TEAM, HEADS),
        jnp.zeros((rows, TEAM, COLS - SMALL_AT), bf),
    ]
    return jnp.moveaxis(jnp.concatenate(pieces, axis=2), 1, 0)


def own_columns(g):
    rows = g.shape[1]

    def joined(at, width):
        return jnp.moveaxis(g[:, :, at : at + width], 0, 1).reshape(rows, TEAM * width)

    def by_group(at):
        part = g[:, :, at : at + HEAD_SIZE].astype(f32).reshape(2, 4, rows, HEAD_SIZE).sum(1)
        return jnp.moveaxis(part, 0, 1).reshape(rows, 2 * HEAD_SIZE).astype(bf)

    state = g[:, :, : 2 * STATE_SIZE].astype(f32).sum(0).astype(bf)
    mix = jnp.concatenate(
        [
            joined(Z_AT, CH),
            joined(X_AT, CH),
            state,
            joined(Q_AT, HEAD_SIZE),
            by_group(Q_AT + HEAD_SIZE),
            by_group(V_AT),
        ],
        axis=1,
    )
    return mix, joined(STEP_AT, HEADS)


def by_layer(blocks):
    own, far, behind, ahead = blocks
    top = lax.axis_index("section") == 0
    return (
        (jnp.where(top, own, behind), jnp.where(top, far, ahead)),
        (jnp.where(top, ahead, own), jnp.where(top, behind, far)),
    )


def in_order(pair):
    first = lax.axis_index("zhi") == 0
    return jnp.where(first, pair[0], pair[1]), jnp.where(first, pair[1], pair[0])


def to_halves(first, second, tiles, top):
    own, away = jnp.where(top, first, second), jnp.where(top, second, first)
    near = swap(away[tiles:], "section").astype(f32)
    cross = lax.ppermute(away[:tiles], RING, [(0, 3), (3, 0), (1, 2), (2, 1)]).astype(f32)
    far = swap(own[:tiles], "zhi").astype(f32)
    total = own[tiles:].astype(f32) + near
    half = total[:tiles] + cross + far
    return half.astype(bf), total[tiles:].astype(bf)


def local(
    layer_input,
    cotangent,
    seq_lengths,
    norm_gains,
    w_mix,
    w_step,
    conv_kernel,
    conv_bias,
    head_params,
    w_out,
    w_gate_up,
    w_down,
):
    section, half = lax.axis_index("section"), lax.axis_index("zhi")
    team = lax.axis_index(("y", "core"))
    top = section == 0
    width = layer_input.shape[-1]

    micro = section

    def of_micro(a):
        return lax.dynamic_index_in_dim(a, micro, 0, False)

    small = jnp.concatenate(
        [norm_gains[0].reshape(-1), conv_kernel[0].reshape(-1), conv_bias[0].reshape(-1)]
    )
    small = jnp.broadcast_to(jnp.pad(small, (0, SMALL - small.shape[0]))[None], (2 * TEAM, SMALL))
    team_axes = ("y", "core")
    x0 = of_micro(layer_input)[0]
    team_x0 = gather_team(x0)
    mix = lax.all_to_all(team_columns(w_mix[0], w_step[0]), team_axes, 0, 0, tiled=True)
    lay = facts(of_micro(seq_lengths)[0], half, team)
    mix = after(mix, lay)
    mix_around = around(mix)
    small, own_heads, cotangent, w_gate_up, w_out = after(
        (small, head_params[0], cotangent, w_gate_up, w_out[0]), mix_around[2], mix_around[3]
    )
    small = lax.all_to_all(small, UNIT_AXES, 0, 0, tiled=True)
    away_small = swap(small, "section")
    away_heads = swap(own_heads, "section")
    up_send = jnp.moveaxis(w_gate_up[0].reshape(BLOCK, 4, TEAM, 128), 2, 0)
    up = lax.all_to_all(up_send.reshape(TEAM, BLOCK, 4 * 128), team_axes, 0, 0, tiled=True)
    w_out, cotangent, up = after((w_out, cotangent, up), mix_around[1])
    out_own = spread_units(w_out.reshape(2, BLOCK, width), lay["info"]).reshape(4 * BLOCK, width)
    out_away = swap(out_own, "section")
    up_around = around(up)
    down_around = around(after(w_down[0], up))
    top_grad = of_micro(cotangent)[0].astype(f32) * lay["valid"]
    team_grad = gather_team(top_grad.astype(bf))
    smalls = []
    for layer in range(2):
        values = jnp.where(top == (layer == 0), small, away_small).astype(f32)
        gains = jnp.moveaxis(values[:, :128].reshape(2 * TEAM, 2, BLOCK), 1, 0).reshape(2, width)
        conv = jnp.moveaxis(values[:, 128:688].reshape(2 * TEAM, KC + 1, 112), 1, 0)
        conv = conv.reshape(KC + 1, XBC)
        conv = jnp.concatenate(
            [conv[:, SPACE_CHANNELS:], lax.dynamic_slice_in_dim(conv, team * CH, CH, 1)], axis=1
        )
        heads = jnp.where(top == (layer == 0), own_heads, away_heads)
        heads = lax.dynamic_slice_in_dim(heads, team * HEADS, HEADS, 1)
        hv = jnp.stack([heads[0], -jnp.exp(heads[1]), heads[2]])
        hv = jnp.pad(hv, ((0, 5), (LANE, 128 - LANE - HEADS)))
        smalls.append(dict(gains=gains, cw=jnp.pad(conv, ((0, 3), (0, 0))), hv=hv))
    team_x0 = after(team_x0, smalls)
    mix_layers = by_layer(mix_around)
    up_layers = by_layer(up_around)
    down_layers = by_layer(down_around)
    weights = []
    for layer in range(2):
        own_layer = top if layer == 0 else jnp.logical_not(top)
        weights.append(
            dict(
                smalls[layer],
                mix=jnp.concatenate([m.reshape(SEQ, COLS) for m in mix_layers[layer]]),
                out=jnp.where(own_layer, out_own, out_away),
                gate_up=jnp.concatenate([u.reshape(SEQ, 2 * HID) for u in up_layers[layer]]),
                down=jnp.concatenate(in_order(down_layers[layer])),
            )
        )
    parts0, kept0 = layer_forward(weights[0], x0, lay, team_x0, (up_around, down_around, team_grad))
    act0 = layer_output(parts0, kept0, lay)
    parts1, kept1 = layer_forward(weights[1], act0, lay, gather_team(act0))
    act1 = layer_output(parts1, kept1, lay)
    grad1, grads1 = layer_backward(weights[1], kept1, top_grad, lay, team_grad, act1)
    low_grad = grad1.astype(bf).astype(f32) * lay["valid"]
    grad0, grads0 = layer_backward(
        weights[0], kept0, low_grad, lay, gather_team(low_grad.astype(bf)), (),
        (grads1["early"], grads1["late"]),
    )

    def placed(first, second):
        other = swap(jnp.where(top, second, first).astype(bf), "section")
        own = jnp.where(top, first, second)
        other = other.astype(own.dtype)
        return jnp.where(top, jnp.stack([own, other]), jnp.stack([other, own]))

    activations = placed(act0, act1)
    input_grads = placed(grad0, grad1)

    early_half, early_out = to_halves(grads0["early"], grads1["early"], EARLY, top)
    early_out = (early_out.astype(f32) + swap(early_out, "zhi").astype(f32)).astype(bf)
    late, _ = to_halves(grads0["late"], grads1["late"], LATE + TEAM, top)
    early = call(
        send_early_kernel,
        [((TEAM, UP_TILES + 16, 16, 128), bf)],
        [],
        lay["info"], early_half, early_out.reshape(4, 8, 16, 128), ties=late,
    )[0]
    early = lax.all_to_all(early, ("y", "core"), 0, 0, tiled=True)
    early = call(
        got_early_kernel,
        [((TEAM * UP_TILES + DOWN_TILES + 16, 16, 128), bf)],
        [],
        lay["info"], early, early_half,
    )[0]
    early = gather_ring(early, "rep")
    count = TEAM * UP_TILES
    up = early[:, :count].reshape(4, TEAM, UP_TILES, 16, 128)
    up = jnp.transpose(up, (0, 3, 2, 1, 4)).reshape(BLOCK, 2 * FF)
    down = early[:, count : count + DOWN_TILES].reshape(4, 2, 8, 16, 128)
    down = jnp.transpose(down, (0, 1, 3, 2, 4)).reshape(128, width)
    out = early[:, count + DOWN_TILES :].reshape(4, 2, 8, 16, 128)
    out = jnp.transpose(out, (1, 0, 3, 2, 4)).reshape(128, width)

    late = jnp.concatenate(
        [late[:LATE].reshape(TEAM, MIX_TILES, 16, 128), late[LATE:].reshape(TEAM, 1, 16, 128)], axis=1
    )
    late = lax.all_to_all(late, ("y", "core"), 0, 0, tiled=True)
    mix, step = own_columns(jnp.moveaxis(late[:, :MIX_TILES], 1, 2).reshape(TEAM, 16, COLS))
    values = jnp.moveaxis(late[:, MIX_TILES], 0, 1).reshape(16, TEAM * 128)
    step = jnp.pad(step, ((0, 0), (0, 128 - MIXER_HEADS)))
    mix = gather_ring(jnp.concatenate([mix, step, values], axis=1), "rep")
    values = mix[:, :, w_mix.shape[2] + 128 :].reshape(4, 16, TEAM, 128).astype(f32)
    gains = values[0, :2, :, :BLOCK].sum(1)
    heads = values[0, 2:5, :, LANE : LANE + HEADS].reshape(3, MIXER_HEADS)
    state = values[1].sum(1).reshape(16, 128)
    state = jnp.concatenate([state[: KC + 1], state[KC + 1 : 2 * (KC + 1)]], axis=1)
    inner = jnp.concatenate(
        [values[2, : KC + 1], values[2, KC + 1 : 2 * (KC + 1), :, : CH - 128]], axis=2
    )
    conv = jnp.concatenate([inner.reshape(KC + 1, SPACE_CHANNELS), state], axis=1)
    owner = lax.axis_index(UNIT_AXES)
    conv = lax.dynamic_slice_in_dim(conv, owner * 112, 112, 1)
    mix = mix.reshape(BLOCK, -1)
    return (
        activations[None, :, None],
        input_grads[None, :, None],
        gains[None],
        mix[:, : w_mix.shape[2]].astype(f32)[None],
        mix[:, w_mix.shape[2] : w_mix.shape[2] + MIXER_HEADS].astype(f32)[None],
        conv[:KC][None],
        conv[KC][None],
        heads[None],
        out.astype(f32)[None],
        up.astype(f32)[None],
        down.astype(f32)[None],
    )


def solution(mesh):
    devices = mesh.devices.reshape(2, 2, 4, 2, 4)
    fine = Mesh(devices, ("section", "zhi", "y", "core", "rep"))
    fsdp = ("zhi", "y", "core")
    in_specs = (
        P(None, "rep", fsdp, None),
        P(None, "rep", fsdp, None),
        P(None, "rep", None),
        P("section", None, fsdp),
        P("section", fsdp, None),
        P("section", fsdp, None),
        P("section", None, fsdp),
        P("section", fsdp),
        P("section", None, None),
        P("section", fsdp, None),
        P("section", fsdp, None),
        P("section", fsdp, None),
    )
    out_specs = (
        P("section", None, "rep", fsdp, None),
        P("section", None, "rep", fsdp, None),
        P("section", None, fsdp),
        P("section", fsdp, None),
        P("section", fsdp, None),
        P("section", None, fsdp),
        P("section", fsdp),
        P("section", None, None),
        P("section", fsdp, None),
        P("section", fsdp, None),
        P("section", fsdp, None),
    )
    return jax.shard_map(local, mesh=fine, in_specs=in_specs, out_specs=out_specs, check_vma=False)
```
